256 devices in a mesh: role: 2 (over x_lo), seq: 128 (over z, x_hi, y, core).
Axes of the slice: x: 4 (x_hi: 2, x_lo: 2; x = x_hi * 2 + x_lo), y: 4, z: 8, core: 2. Of those that a mesh axis runs over, the one named last changes fastest.
Arguments:
- queries: bfloat16 [3072, 4096], P('seq', 'role'), may hold values from -200 to 200
- keys: bfloat16 [3072, 4096], P('seq', 'role'), may hold values from -200 to 200
- values: bfloat16 [3072, 4096], P('seq', 'role'), may hold values from -6 to 6
- q_gain: float32 [4096], P('role'), may hold values from 1.5 to 4
- k_gain: float32 [4096], P('role'), may hold values from 1.5 to 4
Outputs:
- attended: bfloat16 [3072, 4096], P('seq', 'role')
The draws below stay inside these ranges and needn't reach their ends.
All inputs are finite; a program needn't handle non-finite values.
Results may differ from the reference program's by a relative error of at most 0.0049.
The reference program's roundings to bfloat16 on the way (of `weights`) count: a program that leaves them out, or rounds other values in their place, can miss the bound.
Values may be sent and summed in bfloat16 or wider, within the bound.
A program may use at most 64 MiB of HBM per device.

```python
import math
import jax
import jax.numpy as jnp
from jax import lax

HEADS = 32
HEAD_DIM = 128
GRID_H = 30
GRID_W = 52
TOKENS = 3072


def spread(base, row_key, column_key, row_low, row_high):
    feature_count = HEADS * HEAD_DIM
    row_scale = jnp.exp(jax.random.uniform(row_key, (TOKENS, 1), minval=math.log(row_low), maxval=math.log(row_high)))
    column_scale = jnp.exp(jax.random.uniform(column_key, (1, feature_count), minval=0.0, maxval=math.log(10.0)))
    rising = jnp.exp(math.log(3.0) * jnp.arange(feature_count, dtype=jnp.float32)[None, :] / (feature_count - 1))
    return base * row_scale * column_scale * rising


def draw_queries(key, part):
    key = jax.random.fold_in(key, 11)
    base_key, row_key, column_key = jax.random.split(key, 3)
    shape = (TOKENS, HEADS * HEAD_DIM)
    base = jnp.clip(jax.random.normal(base_key, shape), -4.0, 4.0)
    scaled = spread(base, row_key, column_key, 1.0, 10.0)
    return jnp.clip(scaled, -200.0, 200.0).astype(jnp.bfloat16)


def draw_keys(key, part):
    key = jax.random.fold_in(key, 12)
    base_key, row_key, column_key = jax.random.split(key, 3)
    shape = (TOKENS, HEADS * HEAD_DIM)
    base = jnp.clip(jax.random.normal(base_key, shape), -4.0, 4.0)
    scaled = spread(base, row_key, column_key, 1.0, 10.0)
    return jnp.clip(scaled, -200.0, 200.0).astype(jnp.bfloat16)


def block_levels(key, shape, cuts, least, largest):
    gain, own = 1.0, jax.random.fold_in(key, 6)
    for dim, blocks in cuts:
        heights = jnp.exp(jax.random.uniform(jax.random.fold_in(own, dim), (blocks,), jnp.float32, least / len(cuts), largest / len(cuts)))
        gain = gain * jnp.repeat(heights, shape[dim] // blocks).reshape([-1 if axis == dim else 1 for axis in range(len(shape))])
    return gain


def gaussian(stream_key, shape, scale, limit, cuts=(), kind=jnp.bfloat16):
    drawn = scale * jax.random.normal(stream_key, shape, jnp.float32)
    if cuts:
        drawn = drawn * block_levels(stream_key, shape, cuts, -0.22, 0.18)
    return jnp.clip(drawn, -limit, limit).astype(kind)


def setup_inputs(seed: int = 0) -> dict:
    arg_keys = jax.random.split(jax.random.key(seed), 6)
    queries = draw_queries(jax.random.fold_in(arg_keys[5], 71), 0)
    keys = draw_keys(jax.random.fold_in(arg_keys[5], 71), 0)
    values = gaussian(arg_keys[2], (TOKENS, HEADS * HEAD_DIM), 1.0, 6.0, ((0, 128), (1, 2)))
    q_gain = jnp.clip(jnp.exp(math.log(4.0) - 0.98082925 * jax.random.uniform(arg_keys[3], (HEADS * HEAD_DIM,), jnp.float32) ** block_levels(arg_keys[3], (HEADS * HEAD_DIM,), ((0, 2),), -0.2, 0.2)), 1.5, 4.0)
    k_gain = jnp.clip(jnp.exp(math.log(4.0) - 0.98082925 * jax.random.uniform(arg_keys[4], (HEADS * HEAD_DIM,), jnp.float32) ** block_levels(arg_keys[4], (HEADS * HEAD_DIM,), ((0, 2),), -0.2, 0.2)), 1.5, 4.0)
    return dict(queries=queries, keys=keys, values=values, q_gain=q_gain, k_gain=k_gain)


def pair_angles(positions):
    half_dim = HEAD_DIM // 2
    row_pairs = HEAD_DIM // 6
    time_pairs = half_dim - 2 * row_pairs
    frame_ids = positions // (GRID_H * GRID_W)
    row_ids = positions // GRID_W % GRID_H
    column_ids = positions % GRID_W
    pair_ids = jnp.arange(half_dim, dtype=jnp.int32)
    pair_float = pair_ids.astype(jnp.float32)
    in_frames = pair_ids < time_pairs
    in_rows = (pair_ids >= time_pairs) & (pair_ids < time_pairs + row_pairs)
    local_ids = jnp.where(in_frames, pair_float, jnp.where(in_rows, pair_float - time_pairs, pair_float - time_pairs - row_pairs))
    span_width = jnp.where(in_frames, jnp.float32(2 * time_pairs), jnp.float32(2 * row_pairs))
    frequency = jnp.exp(-jnp.log(jnp.float32(10000.0)) * 2.0 * local_ids / span_width)
    coordinate = jnp.where(in_frames[None, :], frame_ids[:, None], jnp.where(in_rows[None, :], row_ids[:, None], column_ids[:, None]))
    return coordinate.astype(jnp.float32) * frequency[None, :]

def rotate(stacked, angles):
    half_dim = HEAD_DIM // 2
    cosine = jnp.cos(angles)[:, None, :]
    sine_part = jnp.sin(angles)[:, None, :]
    front_half = stacked[..., :half_dim]
    back_half = stacked[..., half_dim:]
    return jnp.concatenate([front_half * cosine - back_half * sine_part, front_half * sine_part + back_half * cosine], axis=-1)

def attend(query_block, key_head, value_head):
    scores = lax.dot_general(query_block, key_head, (((1,), (1,)), ((), ())), preferred_element_type=jnp.float32)
    scores = scores * HEAD_DIM ** (-0.5)
    row_top = lax.optimization_barrier(jnp.max(scores, axis=1, keepdims=True))
    exponents = jnp.exp(scores - row_top)
    denominators = lax.optimization_barrier(jnp.sum(exponents, axis=1, keepdims=True))
    weights = exponents.astype(jnp.bfloat16)
    mixed = jnp.dot(weights, value_head, preferred_element_type=jnp.float32)
    return (mixed / denominators).astype(jnp.bfloat16)

def reference(queries, keys, values, q_gain, k_gain):
    token_count = queries.shape[0]
    feature_count = HEADS * HEAD_DIM
    positions = jnp.arange(token_count, dtype=jnp.int32)
    angles = pair_angles(positions)

    def prepare(stacked, gain_row):
        as_float = stacked.astype(jnp.float32)
        total_sq = lax.optimization_barrier(jnp.sum(as_float * as_float, axis=1))
        normed = as_float * lax.rsqrt(total_sq / feature_count + 1e-06)[:, None] * gain_row[None, :]
        rotated = rotate(normed.reshape(token_count, HEADS, HEAD_DIM), angles)
        return rotated.astype(jnp.bfloat16)
    q_rot = prepare(queries, q_gain).transpose(1, 0, 2)
    k_rot = prepare(keys, k_gain).transpose(1, 0, 2)
    v_heads = values.reshape(token_count, HEADS, HEAD_DIM).transpose(1, 0, 2)
    block_rows = 512 if token_count % 512 == 0 else token_count
    block_count = token_count // block_rows

    def one_head(operands):
        q_head, k_head, v_head = operands

        def one_block(query_block):
            return attend(query_block, k_head, v_head)
        outputs = lax.map(one_block, q_head.reshape(block_count, block_rows, HEAD_DIM))
        return outputs.reshape(token_count, HEAD_DIM)
    heads_out = lax.map(one_head, (q_rot, k_rot, v_heads))
    return heads_out.transpose(1, 0, 2).reshape(token_count, feature_count)
```

```python
import math

import jax
import jax.numpy as jnp
from jax import lax
from jax.experimental import pallas as pl
from jax.experimental.pallas import tpu as pltpu
from jax.sharding import PartitionSpec as P

HEADS = 32
HEAD_DIM = 128
GRID_H = 30
GRID_W = 52
CORES = 2
RING = 4
GROUP = CORES * RING
MESH = pl.DeviceIdType.MESH


def angle_tables(first, rows):
    half_dim = HEAD_DIM // 2
    row_pairs = HEAD_DIM // 6
    time_pairs = half_dim - 2 * row_pairs
    lane = lax.broadcasted_iota(jnp.int32, (rows, HEAD_DIM), 1)
    pair = jnp.where(lane < half_dim, lane, lane - half_dim).astype(jnp.float32)
    position = (first + lax.broadcasted_iota(jnp.int32, (rows, HEAD_DIM), 0)).astype(jnp.float32)
    grid_row = jnp.floor((position + 0.5) / GRID_W)
    column = position - GRID_W * grid_row
    frame = jnp.floor((grid_row + 0.5) / GRID_H)
    row = grid_row - GRID_H * frame
    in_frames = pair < time_pairs
    in_rows = jnp.logical_and(pair >= time_pairs, pair < time_pairs + row_pairs)
    local = jnp.where(in_frames, pair, jnp.where(in_rows, pair - time_pairs, pair - time_pairs - row_pairs))
    width = jnp.where(in_frames, jnp.float32(2 * time_pairs), jnp.float32(2 * row_pairs))
    frequency = jnp.exp(-jnp.float32(math.log(10000.0)) * 2.0 * local / width)
    coordinate = jnp.where(in_frames, frame, jnp.where(in_rows, row, column))
    angle = coordinate * frequency
    sine = jnp.sin(angle)
    return jnp.cos(angle), jnp.where(lane < half_dim, -sine, sine)


def kernel(
    q_hbm, k_hbm, v_hbm, q_gain, k_gain, out_hbm,
    q_in, k_in, sums, q_send, k_send, q_land, k_all, v_all, out_send,
    in_sem, sum_sem, a_send, a_recv, g_send, g_recv, o_send, o_recv,
):
    role = lax.axis_index("role")
    seq = lax.axis_index("seq")
    tokens = q_in.shape[0]
    heads = q_send.shape[0]
    keys = heads * tokens
    mine = seq // GROUP
    place = seq % GROUP
    y = place // CORES
    core = place % CORES

    def at_place(other_y, other_core):
        return (role, mine * GROUP + lax.rem(other_y, RING) * CORES + other_core)

    sibling = at_place(y, 1 - core)
    after = at_place(y + 1, core)
    before = at_place(y + RING - 1, core)
    partner = (1 - role, seq)

    def peer(index):
        return (role, index * GROUP + place)

    q_copy = pltpu.make_async_copy(q_hbm, q_in, in_sem.at[0])
    k_copy = pltpu.make_async_copy(k_hbm, k_in, in_sem.at[1])
    q_copy.start()
    k_copy.start()

    barrier = pltpu.get_barrier_semaphore()

    def greet(step, carry):
        pl.semaphore_signal(barrier, inc=1, device_id=peer(lax.rem(mine + step, heads)), device_id_type=MESH)
        return carry

    for other in (partner, sibling, after, before):
        pl.semaphore_signal(barrier, inc=1, device_id=other, device_id_type=MESH)
    lax.fori_loop(1, heads, greet, 0)
    pl.semaphore_wait(barrier, heads + 3)

    def columns(index):
        return pl.ds(pl.multiple_of(index * HEAD_DIM, HEAD_DIM), HEAD_DIM)

    v_own = pltpu.make_async_copy(v_hbm.at[:, columns(mine)], v_all.at[0, mine], a_recv.at[2])
    v_own.start()

    def send_v(step, carry):
        to = lax.rem(mine + step, heads)
        pltpu.make_async_remote_copy(
            src_ref=v_hbm.at[:, columns(to)], dst_ref=v_all.at[0, mine],
            send_sem=a_send.at[2], recv_sem=a_recv.at[2], device_id=peer(to), device_id_type=MESH,
        ).start()
        return carry

    lax.fori_loop(1, heads, send_v, 0)

    q_copy.wait()
    k_copy.wait()

    def square_sum(ref):
        total = jnp.zeros((tokens, HEAD_DIM), jnp.float32)
        for head in range(heads):
            x = ref[:, head * HEAD_DIM:(head + 1) * HEAD_DIM].astype(jnp.float32)
            total = total + x * x
        return jnp.sum(total, axis=1, keepdims=True)

    lane = lax.broadcasted_iota(jnp.int32, (tokens, HEAD_DIM), 1)
    sums[0] = jnp.where(lane < HEAD_DIM // 2, square_sum(q_in), square_sum(k_in))
    sum_copy = pltpu.make_async_remote_copy(
        src_ref=sums.at[0], dst_ref=sums.at[1], send_sem=sum_sem.at[0], recv_sem=sum_sem.at[1],
        device_id=partner, device_id_type=MESH,
    )
    sum_copy.start()
    cosine, sine = angle_tables(seq * tokens, tokens)
    sum_copy.wait()
    scale = lax.rsqrt((sums[0] + sums[1]) / (HEADS * HEAD_DIM) + 1e-06)

    def prepare(source, factor, gain, target):
        for head in range(heads):
            x = source[:, head * HEAD_DIM:(head + 1) * HEAD_DIM].astype(jnp.float32)
            x = x * factor * gain[head:head + 1, :]
            x = x * cosine + pltpu.roll(x, HEAD_DIM // 2, 1) * sine
            target[head] = x.astype(jnp.bfloat16)

    def send_all(source, target, which):
        own = pltpu.make_async_copy(source.at[mine], target.at[mine], a_recv.at[which])
        own.start()

        def send(step, carry):
            to = lax.rem(mine + step, heads)
            pltpu.make_async_remote_copy(
                src_ref=source.at[to], dst_ref=target.at[mine],
                send_sem=a_send.at[which], recv_sem=a_recv.at[which], device_id=peer(to), device_id_type=MESH,
            ).start()
            return carry

        lax.fori_loop(1, heads, send, 0)

    prepare(k_in, scale[:, HEAD_DIM // 2:HEAD_DIM // 2 + 1], k_gain, k_send)
    send_all(k_send, k_all.at[0], 1)
    prepare(q_in, scale[:, 0:1], q_gain, q_send)
    send_all(q_send, q_land, 0)

    def wait_bytes(ref, sem):
        pltpu.make_async_copy(ref, ref, sem).wait()

    started = []

    def pass_on(array, kind, source, target, device):
        copy = pltpu.make_async_remote_copy(
            src_ref=array.at[source], dst_ref=array.at[target],
            send_sem=g_send.at[kind, target], recv_sem=g_recv.at[kind, target], device_id=device, device_id_type=MESH,
        )
        copy.start()
        started.append(copy)

    def arrived(array, kind, block):
        wait_bytes(array.at[block], g_recv.at[kind, block])

    for array, kind, which in ((v_all, 1, 2), (k_all, 0, 1)):
        wait_bytes(array.at[0], a_recv.at[which])
        pass_on(array, kind, 0, 1, after)
        pass_on(array, kind, 0, 2, before)
        pass_on(array, kind, 0, 4, sibling)

    arrived(v_all, 1, 2)
    pass_on(v_all, 1, 2, 3, before)
    pass_on(v_all, 1, 2, 6, sibling)
    arrived(v_all, 1, 1)
    pass_on(v_all, 1, 1, 5, sibling)

    wait_bytes(q_land, a_recv.at[0])
    query = q_land[...].reshape(keys, HEAD_DIM)
    to_exponent = math.log2(math.e) * HEAD_DIM ** (-0.5)

    def absorb(state, block):
        scores = lax.dot_general(
            query, k_all[block].reshape(keys, HEAD_DIM), (((1,), (1,)), ((), ())), preferred_element_type=jnp.float32
        )
        top = jnp.max(scores, axis=1, keepdims=True)
        if state is not None:
            top = jnp.maximum(top, state[0])
        exponents = jnp.exp2((scores - top) * to_exponent)
        total = jnp.sum(exponents, axis=1, keepdims=True)
        mixed = jnp.dot(
            exponents.astype(jnp.bfloat16), v_all[block].reshape(keys, HEAD_DIM), preferred_element_type=jnp.float32
        )
        if state is not None:
            fading = jnp.exp2((state[0] - top) * to_exponent)
            total = state[1] * fading + total
            mixed = state[2] * fading + mixed
        return top, total, mixed

    state = absorb(None, 0)
    arrived(k_all, 0, 1)
    pass_on(k_all, 0, 1, 3, after)
    pass_on(k_all, 0, 1, 5, sibling)
    arrived(v_all, 1, 4)
    arrived(k_all, 0, 4)
    state = absorb(state, 4)
    state = absorb(state, 1)
    arrived(k_all, 0, 2)
    pass_on(k_all, 0, 2, 6, sibling)
    arrived(v_all, 1, 3)
    pass_on(v_all, 1, 3, 7, sibling)
    state = absorb(state, 2)
    arrived(v_all, 1, 5)
    arrived(k_all, 0, 5)
    state = absorb(state, 5)
    arrived(k_all, 0, 3)
    pass_on(k_all, 0, 3, 7, sibling)
    arrived(v_all, 1, 6)
    arrived(k_all, 0, 6)
    state = absorb(state, 6)
    state = absorb(state, 3)
    arrived(v_all, 1, 7)
    arrived(k_all, 0, 7)
    state = absorb(state, 7)

    out_send[...] = (state[2] / state[1]).astype(jnp.bfloat16).reshape(heads, tokens, HEAD_DIM)
    own_out = pltpu.make_async_copy(out_send.at[mine], out_hbm.at[:, columns(mine)], o_recv)
    own_out.start()

    def send_back(step, carry):
        to = lax.rem(mine + step, heads)
        pltpu.make_async_remote_copy(
            src_ref=out_send.at[to], dst_ref=out_hbm.at[:, columns(mine)],
            send_sem=o_send, recv_sem=o_recv, device_id=peer(to), device_id_type=MESH,
        ).start()
        return carry

    lax.fori_loop(1, heads, send_back, 0)

    for copy in started:
        copy.wait_send()
    rest = pl.ds(0, heads - 1)
    wait_bytes(q_land.at[rest], a_send.at[0])
    wait_bytes(q_land.at[rest], a_send.at[1])
    wait_bytes(q_land.at[rest], a_send.at[2])
    wait_bytes(q_land.at[rest], o_send)
    wait_bytes(out_hbm, o_recv)


def on_device(queries, keys, values, q_gain, k_gain):
    tokens, features = queries.shape
    heads = features // HEAD_DIM
    bf16 = jnp.bfloat16
    anywhere = pl.BlockSpec(memory_space=pl.ANY)
    vmem = pl.BlockSpec(memory_space=pltpu.VMEM)
    return pl.pallas_call(
        kernel,
        out_shape=jax.ShapeDtypeStruct((tokens, features), bf16),
        in_specs=[anywhere, anywhere, anywhere, vmem, vmem],
        out_specs=anywhere,
        scratch_shapes=[
            pltpu.VMEM((tokens, features), bf16),
            pltpu.VMEM((tokens, features), bf16),
            pltpu.VMEM((2, tokens, HEAD_DIM), jnp.float32),
            pltpu.VMEM((heads, tokens, HEAD_DIM), bf16),
            pltpu.VMEM((heads, tokens, HEAD_DIM), bf16),
            pltpu.VMEM((heads, tokens, HEAD_DIM), bf16),
            pltpu.VMEM((GROUP, heads, tokens, HEAD_DIM), bf16),
            pltpu.VMEM((GROUP, heads, tokens, HEAD_DIM), bf16),
            pltpu.VMEM((heads, tokens, HEAD_DIM), bf16),
            pltpu.SemaphoreType.DMA((2,)),
            pltpu.SemaphoreType.DMA((2,)),
            pltpu.SemaphoreType.DMA((3,)),
            pltpu.SemaphoreType.DMA((3,)),
            pltpu.SemaphoreType.DMA((2, GROUP)),
            pltpu.SemaphoreType.DMA((2, GROUP)),
            pltpu.SemaphoreType.DMA,
            pltpu.SemaphoreType.DMA,
        ],
        compiler_params=pltpu.CompilerParams(
            collective_id=0, has_side_effects=True, vmem_limit_bytes=48 * 1024 * 1024
        ),
    )(queries, keys, values, q_gain.reshape(heads, HEAD_DIM), k_gain.reshape(heads, HEAD_DIM))


def solution(mesh):
    in_specs = (P("seq", "role"), P("seq", "role"), P("seq", "role"), P("role"), P("role"))
    out_specs = P("seq", "role")
    return jax.shard_map(
        on_device, mesh=mesh, in_specs=in_specs, out_specs=out_specs, check_vma=False
    )
```

```python
import math

import jax
import jax.numpy as jnp
from jax import lax
from jax.experimental import pallas as pl
from jax.experimental.pallas import tpu as pltpu
from jax.sharding import PartitionSpec as P

HEADS = 32
HEAD_DIM = 128
GRID_H = 30
GRID_W = 52
DEPTH = 8
CORES = 2
RING = 4
PLACES = CORES * RING
BATCH = 4
OFFSETS = (
    (0, 0), (1, 0), (7, 0), (0, 1),
    (2, 0), (6, 0), (1, 1), (7, 1),
    (3, 0), (5, 0), (2, 1), (6, 1),
    (4, 0), (3, 1), (5, 1), (4, 1),
)
MESH = pl.DeviceIdType.MESH


def angle_tables(first, rows):
    half_dim = HEAD_DIM // 2
    row_pairs = HEAD_DIM // 6
    time_pairs = half_dim - 2 * row_pairs
    lane = lax.broadcasted_iota(jnp.int32, (rows, HEAD_DIM), 1)
    pair = jnp.where(lane < half_dim, lane, lane - half_dim).astype(jnp.float32)
    position = (first + lax.broadcasted_iota(jnp.int32, (rows, HEAD_DIM), 0)).astype(jnp.float32)
    grid_row = jnp.floor((position + 0.5) / GRID_W)
    column = position - GRID_W * grid_row
    frame = jnp.floor((grid_row + 0.5) / GRID_H)
    row = grid_row - GRID_H * frame
    in_frames = pair < time_pairs
    in_rows = jnp.logical_and(pair >= time_pairs, pair < time_pairs + row_pairs)
    local = jnp.where(in_frames, pair, jnp.where(in_rows, pair - time_pairs, pair - time_pairs - row_pairs))
    width = jnp.where(in_frames, jnp.float32(2 * time_pairs), jnp.float32(2 * row_pairs))
    frequency = jnp.exp(-jnp.float32(math.log(10000.0)) * 2.0 * local / width)
    coordinate = jnp.where(in_frames, frame, jnp.where(in_rows, row, column))
    angle = coordinate * frequency
    sine = jnp.sin(angle)
    return jnp.cos(angle), jnp.where(lane < half_dim, -sine, sine)


def kernel(
    q_hbm, k_hbm, v_hbm, q_gain_hbm, k_gain_hbm, out_hbm,
    q_in, k_in, q_gain, k_gain, sums, q_send, k_send, q_land, k_all, v_all, out_send,
    in_sem, sum_sem, a_send, a_recv, y_send, y_recv, s_send, s_recv, o_send, o_recv,
):
    role = lax.axis_index("role")
    seq = lax.axis_index("seq")
    tokens = q_in.shape[0]
    heads = q_send.shape[0]
    keys = heads * tokens
    mine = seq // PLACES
    place = seq % PLACES
    z = mine // 2
    x = mine % 2
    y = place // CORES
    core = place % CORES

    loads = [
        pltpu.make_async_copy(source, target, in_sem.at[index])
        for index, (source, target) in enumerate(
            ((q_hbm, q_in), (k_hbm, k_in), (k_gain_hbm, k_gain), (q_gain_hbm, q_gain))
        )
    ]
    for load in loads:
        load.start()

    def home(index):
        dz, dx = OFFSETS[index]
        return lax.rem(z + dz, DEPTH) * 2 + (1 - x if dx else x)

    def server(index):
        dz, dx = OFFSETS[index]
        return lax.rem(z + DEPTH - dz, DEPTH) * 2 + (1 - x if dx else x)

    def peer(index):
        return (role, index * PLACES + place)

    def across(step):
        return (role, mine * PLACES + lax.rem(y + step, RING) * CORES + core)

    sibling = (role, mine * PLACES + y * CORES + 1 - core)
    partner = (1 - role, seq)
    far_first = range(heads - 1, 0, -1)

    barrier = pltpu.get_barrier_semaphore()
    for index in far_first:
        pl.semaphore_signal(barrier, inc=1, device_id=peer(server(index)), device_id_type=MESH)
    for other in (partner, sibling, across(1), across(2), across(3)):
        pl.semaphore_signal(barrier, inc=1, device_id=other, device_id_type=MESH)
    pl.semaphore_wait(barrier, heads + RING)

    def columns(index):
        return pl.ds(pl.multiple_of(index * HEAD_DIM, HEAD_DIM), HEAD_DIM)

    def remote(source, target, send_sem, recv_sem, device):
        pltpu.make_async_remote_copy(
            src_ref=source, dst_ref=target, send_sem=send_sem, recv_sem=recv_sem, device_id=device, device_id_type=MESH
        ).start()

    def wait_bytes(ref, sem):
        pltpu.make_async_copy(ref, ref, sem).wait()

    def exchange(pick, slot, kind):
        for index in far_first:
            to = server(index)
            remote(pick(to), slot(index), a_send.at[kind], a_recv.at[kind, index // BATCH], peer(to))
        pltpu.make_async_copy(pick(mine), slot(0), a_recv.at[kind, 0]).start()

    exchange(lambda to: v_hbm.at[:, columns(to)], lambda i: v_all.at[0, i // BATCH, 0, i % BATCH], 2)

    loads[0].wait()
    loads[1].wait()

    def square_sum(ref):
        total = jnp.zeros((tokens, HEAD_DIM), jnp.float32)
        for head in range(heads):
            rows = ref[:, head * HEAD_DIM:(head + 1) * HEAD_DIM].astype(jnp.float32)
            total = total + rows * rows
        return jnp.sum(total, axis=1, keepdims=True)

    lane = lax.broadcasted_iota(jnp.int32, (tokens, HEAD_DIM), 1)
    sums[0] = jnp.where(lane < HEAD_DIM // 2, square_sum(q_in), square_sum(k_in))
    sum_copy = pltpu.make_async_remote_copy(
        src_ref=sums.at[0], dst_ref=sums.at[1], send_sem=sum_sem.at[0], recv_sem=sum_sem.at[1],
        device_id=partner, device_id_type=MESH,
    )
    sum_copy.start()
    cosine, sine = angle_tables(seq * tokens, tokens)
    loads[2].wait()
    loads[3].wait()
    sum_copy.wait()
    scale = lax.rsqrt((sums[0] + sums[1]) / (HEADS * HEAD_DIM) + 1e-06)

    def prepare(source, factor, gain, target):
        for head in range(heads):
            rows = source[:, head * HEAD_DIM:(head + 1) * HEAD_DIM].astype(jnp.float32)
            rows = rows * factor * gain[head:head + 1, :]
            rows = rows * cosine + pltpu.roll(rows, HEAD_DIM // 2, 1) * sine
            target[head] = rows.astype(jnp.bfloat16)

    prepare(k_in, scale[:, HEAD_DIM // 2:HEAD_DIM // 2 + 1], k_gain, k_send)
    exchange(lambda to: k_send.at[to], lambda i: k_all.at[0, i // BATCH, 0, i % BATCH], 1)
    prepare(q_in, scale[:, 0:1], q_gain, q_send)
    exchange(lambda to: q_send.at[to], lambda i: q_land.at[i], 0)

    for array, kind in ((v_all, 2), (k_all, 1)):
        for batch in range(heads // BATCH):
            wait_bytes(array.at[0, batch, 0], a_recv.at[kind, batch])
            for step in (2, 1, 3):
                remote(
                    array.at[0, batch, 0], array.at[0, batch, step],
                    y_send.at[kind - 1], y_recv.at[kind - 1, batch], across(step),
                )

    def gathered(array, kind, batch):
        wait_bytes(array.at[0, batch, pl.ds(1, RING - 1)], y_recv.at[kind - 1, batch])
        remote(array.at[0, batch], array.at[1, batch], s_send.at[kind - 1], s_recv.at[kind - 1, batch], sibling)

    for batch in range(heads // BATCH):
        gathered(v_all, 2, batch)

    for batch in range(heads // BATCH):
        wait_bytes(q_land.at[pl.ds(batch * BATCH, BATCH)], a_recv.at[0, batch])
    query = q_land[...].reshape(keys, HEAD_DIM)
    to_exponent = math.log2(math.e) * HEAD_DIM ** (-0.5)

    def absorb(state, half, batch):
        if half:
            wait_bytes(v_all.at[1, batch], s_recv.at[1, batch])
            wait_bytes(k_all.at[1, batch], s_recv.at[0, batch])
        scores = lax.dot_general(
            query, k_all[half, batch].reshape(-1, HEAD_DIM), (((1,), (1,)), ((), ())),
            preferred_element_type=jnp.float32,
        )
        top = jnp.max(scores, axis=1, keepdims=True)
        if state is not None:
            top = jnp.maximum(top, state[0])
        exponents = jnp.exp2((scores - top) * to_exponent)
        total = jnp.sum(exponents, axis=1, keepdims=True)
        mixed = jnp.dot(
            exponents.astype(jnp.bfloat16), v_all[half, batch].reshape(-1, HEAD_DIM),
            preferred_element_type=jnp.float32,
        )
        if state is not None:
            fading = jnp.exp2((state[0] - top) * to_exponent)
            total = state[1] * fading + total
            mixed = state[2] * fading + mixed
        return top, total, mixed

    state = None
    for batch in range(heads // BATCH):
        gathered(k_all, 1, batch)
        if batch:
            state = absorb(state, 1, batch - 1)
        state = absorb(state, 0, batch)
    state = absorb(state, 1, heads // BATCH - 1)

    out_send[...] = (state[2] / state[1]).astype(jnp.bfloat16).reshape(heads, tokens, HEAD_DIM)
    for index in far_first:
        remote(out_send.at[index], out_hbm.at[:, columns(mine)], o_send, o_recv, peer(home(index)))
    pltpu.make_async_copy(out_send.at[0], out_hbm.at[:, columns(mine)], o_recv).start()

    for kind in range(3):
        wait_bytes(q_land.at[pl.ds(0, heads - 1)], a_send.at[kind])
    for array, kind in ((k_all, 0), (v_all, 1)):
        wait_bytes(array.at[0, pl.ds(0, RING - 1)], y_send.at[kind])
        wait_bytes(array.at[1], s_send.at[kind])
    wait_bytes(q_land.at[pl.ds(0, heads - 1)], o_send)
    wait_bytes(out_hbm, o_recv)


def on_device(queries, keys, values, q_gain, k_gain):
    tokens, features = queries.shape
    heads = features // HEAD_DIM
    batches = heads // BATCH
    bf16 = jnp.bfloat16
    in_hbm = pl.BlockSpec(memory_space=pltpu.HBM)
    return pl.pallas_call(
        kernel,
        out_shape=jax.ShapeDtypeStruct((tokens, features), bf16),
        in_specs=[in_hbm] * 5,
        out_specs=pl.BlockSpec(memory_space=pltpu.VMEM),
        scratch_shapes=[
            pltpu.VMEM((tokens, features), bf16),
            pltpu.VMEM((tokens, features), bf16),
            pltpu.VMEM((heads, HEAD_DIM), jnp.float32),
            pltpu.VMEM((heads, HEAD_DIM), jnp.float32),
            pltpu.VMEM((2, tokens, HEAD_DIM), jnp.float32),
            pltpu.VMEM((heads, tokens, HEAD_DIM), bf16),
            pltpu.VMEM((heads, tokens, HEAD_DIM), bf16),
            pltpu.VMEM((heads, tokens, HEAD_DIM), bf16),
            pltpu.VMEM((CORES, batches, RING, BATCH, tokens, HEAD_DIM), bf16),
            pltpu.VMEM((CORES, batches, RING, BATCH, tokens, HEAD_DIM), bf16),
            pltpu.VMEM((heads, tokens, HEAD_DIM), bf16),
            pltpu.SemaphoreType.DMA((4,)),
            pltpu.SemaphoreType.DMA((2,)),
            pltpu.SemaphoreType.DMA((3,)),
            pltpu.SemaphoreType.DMA((3, batches)),
            pltpu.SemaphoreType.DMA((2,)),
            pltpu.SemaphoreType.DMA((2, batches)),
            pltpu.SemaphoreType.DMA((2,)),
            pltpu.SemaphoreType.DMA((2, batches)),
            pltpu.SemaphoreType.DMA,
            pltpu.SemaphoreType.DMA,
        ],
        compiler_params=pltpu.CompilerParams(
            collective_id=0, has_side_effects=True, vmem_limit_bytes=40 * 1024 * 1024
        ),
    )(*(
        pltpu.with_memory_space_constraint(array, pltpu.HBM)
        for array in (queries, keys, values, q_gain.reshape(heads, HEAD_DIM), k_gain.reshape(heads, HEAD_DIM))
    ))


def solution(mesh):
    in_specs = (P("seq", "role"), P("seq", "role"), P("seq", "role"), P("role"), P("role"))
    out_specs = P("seq", "role")
    return jax.shard_map(
        on_device, mesh=mesh, in_specs=in_specs, out_specs=out_specs, check_vma=False
    )
```

```python
import math

import jax
import jax.numpy as jnp
from jax import lax
from jax.experimental import pallas as pl
from jax.experimental.pallas import tpu as pltpu
from jax.sharding import PartitionSpec as P

HEADS = 32
HEAD_DIM = 128
GRID_H = 30
GRID_W = 52
DEPTH = 8
CORES = 2
RING = 4
PLACES = CORES * RING
BATCH = 4
OFFSETS = (
    (0, 0), (1, 0), (7, 0), (0, 1),
    (2, 0), (6, 0), (1, 1), (7, 1),
    (3, 0), (5, 0), (2, 1), (6, 1),
    (4, 0), (3, 1), (5, 1), (4, 1),
)
PIECE = 2
RELAY = (None, (0, 0, 0, 0), (1, 2, 1, 2))
MESH = pl.DeviceIdType.MESH


def angle_tables(first, rows):
    half_dim = HEAD_DIM // 2
    row_pairs = HEAD_DIM // 6
    time_pairs = half_dim - 2 * row_pairs
    lane = lax.broadcasted_iota(jnp.int32, (rows, HEAD_DIM), 1)
    pair = jnp.where(lane < half_dim, lane, lane - half_dim).astype(jnp.float32)
    position = (first + lax.broadcasted_iota(jnp.int32, (rows, HEAD_DIM), 0)).astype(jnp.float32)
    grid_row = jnp.floor((position + 0.5) / GRID_W)
    column = position - GRID_W * grid_row
    frame = jnp.floor((grid_row + 0.5) / GRID_H)
    row = grid_row - GRID_H * frame
    in_frames = pair < time_pairs
    in_rows = jnp.logical_and(pair >= time_pairs, pair < time_pairs + row_pairs)
    local = jnp.where(in_frames, pair, jnp.where(in_rows, pair - time_pairs, pair - time_pairs - row_pairs))
    width = jnp.where(in_frames, jnp.float32(2 * time_pairs), jnp.float32(2 * row_pairs))
    frequency = jnp.exp(-jnp.float32(math.log(10000.0)) * 2.0 * local / width)
    coordinate = jnp.where(in_frames, frame, jnp.where(in_rows, row, column))
    angle = coordinate * frequency
    sine = jnp.sin(angle)
    return jnp.cos(angle), jnp.where(lane < half_dim, -sine, sine)


def kernel(
    q_hbm, k_hbm, v_hbm, q_gain_hbm, k_gain_hbm, out_hbm,
    q_in, k_in, q_gain, k_gain, sums, q_send, k_send, q_land, k_all, v_all, out_send,
    in_sem, sum_sem, a_send, a_recv, y_send, y_recv, s_send, s_recv, o_send, o_recv,
):
    role = lax.axis_index("role")
    seq = lax.axis_index("seq")
    tokens = q_in.shape[0]
    heads = q_send.shape[0]
    keys = heads * tokens
    mine = seq // PLACES
    place = seq % PLACES
    z = mine // 2
    x = mine % 2
    y = place // CORES
    core = place % CORES

    loads = [
        pltpu.make_async_copy(source, target, in_sem.at[index])
        for index, (source, target) in enumerate(
            ((q_hbm, q_in), (k_hbm, k_in), (k_gain_hbm, k_gain), (q_gain_hbm, q_gain))
        )
    ]
    for load in loads:
        load.start()

    def home(index):
        dz, dx = OFFSETS[index]
        return lax.rem(z + dz, DEPTH) * 2 + (1 - x if dx else x)

    def server(index):
        dz, dx = OFFSETS[index]
        return lax.rem(z + DEPTH - dz, DEPTH) * 2 + (1 - x if dx else x)

    def peer(index):
        return (role, index * PLACES + place)

    def across(step):
        return (role, mine * PLACES + lax.rem(y + step, RING) * CORES + core)

    sibling = (role, mine * PLACES + y * CORES + 1 - core)
    partner = (1 - role, seq)
    far_first = range(heads - 1, 0, -1)

    barrier = pltpu.get_barrier_semaphore()
    for index in far_first:
        pl.semaphore_signal(barrier, inc=1, device_id=peer(server(index)), device_id_type=MESH)
    for other in (partner, sibling, across(1), across(2), across(3)):
        pl.semaphore_signal(barrier, inc=1, device_id=other, device_id_type=MESH)
    pl.semaphore_wait(barrier, heads + RING)

    def columns(index):
        return pl.ds(pl.multiple_of(index * HEAD_DIM, HEAD_DIM), HEAD_DIM)

    def remote(source, target, send_sem, recv_sem, device):
        pltpu.make_async_remote_copy(
            src_ref=source, dst_ref=target, send_sem=send_sem, recv_sem=recv_sem, device_id=device, device_id_type=MESH
        ).start()

    def wait_bytes(ref, sem):
        pltpu.make_async_copy(ref, ref, sem).wait()

    def exchange(pick, slot, kind):
        for index in far_first:
            to = server(index)
            remote(pick(to), slot(index), a_send.at[kind], a_recv.at[kind, index // PIECE], peer(to))
        pltpu.make_async_copy(pick(mine), slot(0), a_recv.at[kind, 0]).start()

    exchange(lambda to: v_hbm.at[:, columns(to)], lambda i: v_all.at[0, i // BATCH, 0, i % BATCH], 2)

    loads[0].wait()
    loads[1].wait()

    def square_sum(ref):
        total = jnp.zeros((tokens, HEAD_DIM), jnp.float32)
        for head in range(heads):
            rows = ref[:, head * HEAD_DIM:(head + 1) * HEAD_DIM].astype(jnp.float32)
            total = total + rows * rows
        return jnp.sum(total, axis=1, keepdims=True)

    lane = lax.broadcasted_iota(jnp.int32, (tokens, HEAD_DIM), 1)
    sums[0] = jnp.where(lane < HEAD_DIM // 2, square_sum(q_in), square_sum(k_in))
    sum_copy = pltpu.make_async_remote_copy(
        src_ref=sums.at[0], dst_ref=sums.at[1], send_sem=sum_sem.at[0], recv_sem=sum_sem.at[1],
        device_id=partner, device_id_type=MESH,
    )
    sum_copy.start()
    cosine, sine = angle_tables(seq * tokens, tokens)
    loads[2].wait()
    loads[3].wait()
    sum_copy.wait()
    scale = lax.rsqrt((sums[0] + sums[1]) / (HEADS * HEAD_DIM) + 1e-06)

    def prepare(source, factor, gain, target):
        for head in range(heads):
            rows = source[:, head * HEAD_DIM:(head + 1) * HEAD_DIM].astype(jnp.float32)
            rows = rows * factor * gain[head:head + 1, :]
            rows = rows * cosine + pltpu.roll(rows, HEAD_DIM // 2, 1) * sine
            target[head] = rows.astype(jnp.bfloat16)

    prepare(k_in, scale[:, HEAD_DIM // 2:HEAD_DIM // 2 + 1], k_gain, k_send)
    exchange(lambda to: k_send.at[to], lambda i: k_all.at[0, i // BATCH, 0, i % BATCH], 1)
    prepare(q_in, scale[:, 0:1], q_gain, q_send)
    exchange(lambda to: q_send.at[to], lambda i: q_land.at[i], 0)

    batches = heads // BATCH

    def spread(array, kind, batch):
        for piece in range(batch * BATCH // PIECE, (batch + 1) * BATCH // PIECE):
            rows = pl.ds(piece * PIECE % BATCH, PIECE)
            own = array.at[0, batch, 0, rows]
            wait_bytes(own, a_recv.at[kind, piece])
            for step, slot in ((2, 3), (1, 1), (3, 2)) if RELAY[kind][batch] == 0 else ((1, 1), (3, 2)):
                remote(
                    own, array.at[0, batch, slot, rows],
                    y_send.at[kind - 1], y_recv.at[kind - 1, batch, slot - 1], across(step),
                )

    def relay(array, kind, batch):
        slot = RELAY[kind][batch]
        if slot:
            wait_bytes(array.at[0, batch, slot], y_recv.at[kind - 1, batch, slot - 1])
            remote(
                array.at[0, batch, slot], array.at[0, batch, 3],
                y_send.at[kind - 1], y_recv.at[kind - 1, batch, 2], across(1 if slot == 1 else 3),
            )

    def gathered(array, kind, batch):
        for slot in (1, 2, 3):
            if slot != RELAY[kind][batch]:
                wait_bytes(array.at[0, batch, slot], y_recv.at[kind - 1, batch, slot - 1])
        remote(array.at[0, batch], array.at[1, batch], s_send.at[kind - 1], s_recv.at[kind - 1, batch], sibling)

    for batch in range(batches):
        spread(v_all, 2, batch)
    for batch in range(batches):
        spread(k_all, 1, batch)
        relay(v_all, 2, batch)

    for piece in range(heads // PIECE):
        wait_bytes(q_land.at[pl.ds(piece * PIECE, PIECE)], a_recv.at[0, piece])
    query = q_land[...].reshape(keys, HEAD_DIM)
    to_exponent = math.log2(math.e) * HEAD_DIM ** (-0.5)

    def absorb(state, half, batch):
        if half:
            wait_bytes(v_all.at[1, batch], s_recv.at[1, batch])
            wait_bytes(k_all.at[1, batch], s_recv.at[0, batch])
        scores = lax.dot_general(
            query, k_all[half, batch].reshape(-1, HEAD_DIM), (((1,), (1,)), ((), ())),
            preferred_element_type=jnp.float32,
        )
        top = jnp.max(scores, axis=1, keepdims=True)
        if state is not None:
            top = jnp.maximum(top, state[0])
        exponents = jnp.exp2((scores - top) * to_exponent)
        total = jnp.sum(exponents, axis=1, keepdims=True)
        mixed = jnp.dot(
            exponents.astype(jnp.bfloat16), v_all[half, batch].reshape(-1, HEAD_DIM),
            preferred_element_type=jnp.float32,
        )
        if state is not None:
            fading = jnp.exp2((state[0] - top) * to_exponent)
            total = state[1] * fading + total
            mixed = state[2] * fading + mixed
        return top, total, mixed

    state = None
    for batch in range(batches):
        for array, kind in ((k_all, 1), (v_all, 2)):
            gathered(array, kind, batch)
        if batch:
            state = absorb(state, 1, batch - 1)
        state = absorb(state, 0, batch)
    state = absorb(state, 1, batches - 1)

    out_send[...] = (state[2] / state[1]).astype(jnp.bfloat16).reshape(heads, tokens, HEAD_DIM)
    for index in far_first:
        remote(out_send.at[index], out_hbm.at[:, columns(mine)], o_send, o_recv, peer(home(index)))
    pltpu.make_async_copy(out_send.at[0], out_hbm.at[:, columns(mine)], o_recv).start()

    for kind in range(3):
        wait_bytes(q_land.at[pl.ds(0, heads - 1)], a_send.at[kind])
    for array, kind in ((k_all, 0), (v_all, 1)):
        wait_bytes(array.at[0, pl.ds(0, RING - 1)], y_send.at[kind])
        wait_bytes(array.at[1], s_send.at[kind])
    wait_bytes(q_land.at[pl.ds(0, heads - 1)], o_send)
    wait_bytes(out_hbm, o_recv)


def on_device(queries, keys, values, q_gain, k_gain):
    tokens, features = queries.shape
    heads = features // HEAD_DIM
    batches = heads // BATCH
    bf16 = jnp.bfloat16
    in_hbm = pl.BlockSpec(memory_space=pltpu.HBM)
    return pl.pallas_call(
        kernel,
        out_shape=jax.ShapeDtypeStruct((tokens, features), bf16),
        in_specs=[in_hbm] * 5,
        out_specs=pl.BlockSpec(memory_space=pltpu.VMEM),
        scratch_shapes=[
            pltpu.VMEM((tokens, features), bf16),
            pltpu.VMEM((tokens, features), bf16),
            pltpu.VMEM((heads, HEAD_DIM), jnp.float32),
            pltpu.VMEM((heads, HEAD_DIM), jnp.float32),
            pltpu.VMEM((2, tokens, HEAD_DIM), jnp.float32),
            pltpu.VMEM((heads, tokens, HEAD_DIM), bf16),
            pltpu.VMEM((heads, tokens, HEAD_DIM), bf16),
            pltpu.VMEM((heads, tokens, HEAD_DIM), bf16),
            pltpu.VMEM((CORES, batches, RING, BATCH, tokens, HEAD_DIM), bf16),
            pltpu.VMEM((CORES, batches, RING, BATCH, tokens, HEAD_DIM), bf16),
            pltpu.VMEM((heads, tokens, HEAD_DIM), bf16),
            pltpu.SemaphoreType.DMA((4,)),
            pltpu.SemaphoreType.DMA((2,)),
            pltpu.SemaphoreType.DMA((3,)),
            pltpu.SemaphoreType.DMA((3, heads // PIECE)),
            pltpu.SemaphoreType.DMA((2,)),
            pltpu.SemaphoreType.DMA((2, batches, RING - 1)),
            pltpu.SemaphoreType.DMA((2,)),
            pltpu.SemaphoreType.DMA((2, batches)),
            pltpu.SemaphoreType.DMA,
            pltpu.SemaphoreType.DMA,
        ],
        compiler_params=pltpu.CompilerParams(
            collective_id=0, has_side_effects=True, vmem_limit_bytes=40 * 1024 * 1024
        ),
    )(*(
        pltpu.with_memory_space_constraint(array, pltpu.HBM)
        for array in (queries, keys, values, q_gain.reshape(heads, HEAD_DIM), k_gain.reshape(heads, HEAD_DIM))
    ))


def solution(mesh):
    in_specs = (P("seq", "role"), P("seq", "role"), P("seq", "role"), P("role"), P("role"))
    out_specs = P("seq", "role")
    return jax.shard_map(
        on_device, mesh=mesh, in_specs=in_specs, out_specs=out_specs, check_vma=False
    )
```

```python
import functools
import math

import jax
import jax.numpy as jnp
from jax import lax
from jax.experimental import pallas as pl
from jax.experimental.pallas import tpu as pltpu
from jax.sharding import PartitionSpec as P

HEADS = 32
HEAD_DIM = 128
GRID_H = 30
GRID_W = 52
DEPTH = 8
CORES = 2
RING = 4
PLACES = CORES * RING
BATCH = 4
OFFSETS = (
    (0, 0), (1, 0), (7, 0), (0, 1),
    (2, 0), (6, 0), (1, 1), (7, 1),
    (3, 0), (5, 0), (2, 1), (6, 1),
    (4, 0), (3, 1), (5, 1), (4, 1),
)
PIECE = 2
RELAY = (None, (0, 0, 0, 0), (1, 2, 1, 2))
MESH = pl.DeviceIdType.MESH


def angle_tables(first, rows):
    half_dim = HEAD_DIM // 2
    row_pairs = HEAD_DIM // 6
    time_pairs = half_dim - 2 * row_pairs
    lane = lax.broadcasted_iota(jnp.int32, (rows, HEAD_DIM), 1)
    pair = jnp.where(lane < half_dim, lane, lane - half_dim).astype(jnp.float32)
    position = (first + lax.broadcasted_iota(jnp.int32, (rows, HEAD_DIM), 0)).astype(jnp.float32)
    grid_row = jnp.floor((position + 0.5) / GRID_W)
    column = position - GRID_W * grid_row
    frame = jnp.floor((grid_row + 0.5) / GRID_H)
    row = grid_row - GRID_H * frame
    in_frames = pair < time_pairs
    in_rows = jnp.logical_and(pair >= time_pairs, pair < time_pairs + row_pairs)
    local = jnp.where(in_frames, pair, jnp.where(in_rows, pair - time_pairs, pair - time_pairs - row_pairs))
    width = jnp.where(in_frames, jnp.float32(2 * time_pairs), jnp.float32(2 * row_pairs))
    frequency = jnp.exp(-jnp.float32(math.log(10000.0)) * 2.0 * local / width)
    coordinate = jnp.where(in_frames, frame, jnp.where(in_rows, row, column))
    angle = coordinate * frequency
    sine = jnp.sin(angle)
    return jnp.cos(angle), jnp.where(lane < half_dim, -sine, sine)


def kernel(
    q_hbm, k_hbm, v_hbm, q_gain_hbm, k_gain_hbm, out_hbm,
    q_in, k_in, v_in, q_gain, k_gain, sums, q_send, k_send, q_land, k_all, v_all, out_send,
    in_sem, sum_sem, a_send, a_recv, y_send, y_recv, s_send, s_recv, o_send, o_recv,
):
    role = lax.axis_index("role")
    seq = lax.axis_index("seq")
    tokens = q_in.shape[0]
    heads = q_send.shape[0]
    keys = heads * tokens
    mine = seq // PLACES
    place = seq % PLACES
    z = mine // 2
    x = mine % 2
    y = place // CORES
    core = place % CORES

    loads = [
        pltpu.make_async_copy(source, target, in_sem.at[index])
        for index, (source, target) in enumerate(
            ((q_hbm, q_in), (k_hbm, k_in), (k_gain_hbm, k_gain), (q_gain_hbm, q_gain), (v_hbm, v_in))
        )
    ]
    for load in loads:
        load.start()

    def home(index):
        dz, dx = OFFSETS[index]
        return lax.rem(z + dz, DEPTH) * 2 + (1 - x if dx else x)

    def server(index):
        dz, dx = OFFSETS[index]
        return lax.rem(z + DEPTH - dz, DEPTH) * 2 + (1 - x if dx else x)

    def peer(index):
        return (role, index * PLACES + place)

    def across(step):
        return (role, mine * PLACES + lax.rem(y + step, RING) * CORES + core)

    sibling = (role, mine * PLACES + y * CORES + 1 - core)
    partner = (1 - role, seq)
    far_first = range(heads - 1, 0, -1)
    servers = [server(index) for index in range(heads)]
    homes = [home(index) for index in range(heads)]
    server_peers = [peer(index) for index in servers]
    home_peers = [peer(index) for index in homes]
    ring = [across(step) for step in range(RING)]

    barrier = pltpu.get_barrier_semaphore()
    for index in far_first:
        pl.semaphore_signal(barrier, inc=1, device_id=server_peers[index], device_id_type=MESH)
    for other in (partner, sibling, ring[1], ring[2], ring[3]):
        pl.semaphore_signal(barrier, inc=1, device_id=other, device_id_type=MESH)
    loads[0].wait()
    loads[1].wait()

    def square_sum(ref):
        total = jnp.zeros((tokens, HEAD_DIM), jnp.float32)
        for head in range(heads):
            rows = ref[:, head * HEAD_DIM:(head + 1) * HEAD_DIM].astype(jnp.float32)
            total = total + rows * rows
        return jnp.sum(total, axis=1, keepdims=True)

    lane = lax.broadcasted_iota(jnp.int32, (tokens, HEAD_DIM), 1)
    sums[0] = jnp.where(lane < HEAD_DIM // 2, square_sum(q_in), square_sum(k_in))
    cosine, sine = angle_tables(seq * tokens, tokens)
    loads[2].wait()
    loads[3].wait()
    loads[4].wait()
    pl.semaphore_wait(barrier, heads + RING)

    def columns(index):
        return pl.ds(pl.multiple_of(index * HEAD_DIM, HEAD_DIM), HEAD_DIM)

    def remote(source, target, send_sem, recv_sem, device):
        pltpu.make_async_remote_copy(
            src_ref=source, dst_ref=target, send_sem=send_sem, recv_sem=recv_sem, device_id=device, device_id_type=MESH
        ).start()

    def wait_bytes(ref, sem):
        pltpu.make_async_copy(ref, ref, sem).wait()

    def exchange(pick, slot, kind):
        for index in far_first:
            remote(
                pick(servers[index]), slot(index), a_send.at[kind], a_recv.at[kind, index // PIECE],
                server_peers[index],
            )
        pltpu.make_async_copy(pick(mine), slot(0), a_recv.at[kind, 0]).start()

    exchange(lambda to: v_in.at[:, columns(to)], lambda i: v_all.at[0, i // BATCH, 0, i % BATCH], 2)

    sum_copy = pltpu.make_async_remote_copy(
        src_ref=sums.at[0], dst_ref=sums.at[1], send_sem=sum_sem.at[0], recv_sem=sum_sem.at[1],
        device_id=partner, device_id_type=MESH,
    )
    sum_copy.start()
    sum_copy.wait()
    scale = lax.rsqrt((sums[0] + sums[1]) / (HEADS * HEAD_DIM) + 1e-06)

    def prepare(source, factor, gain, target):
        for head in range(heads):
            rows = source[:, head * HEAD_DIM:(head + 1) * HEAD_DIM].astype(jnp.float32)
            rows = rows * factor * gain[head:head + 1, :]
            rows = rows * cosine + pltpu.roll(rows, HEAD_DIM // 2, 1) * sine
            target[head] = rows.astype(jnp.bfloat16)

    prepare(k_in, scale[:, HEAD_DIM // 2:HEAD_DIM // 2 + 1], k_gain, k_send)
    exchange(lambda to: k_send.at[to], lambda i: k_all.at[0, i // BATCH, 0, i % BATCH], 1)
    prepare(q_in, scale[:, 0:1], q_gain, q_send)
    exchange(lambda to: q_send.at[to], lambda i: q_land.at[i], 0)

    batches = heads // BATCH

    def spread(array, kind, batch):
        for piece in range(batch * BATCH // PIECE, (batch + 1) * BATCH // PIECE):
            rows = pl.ds(piece * PIECE % BATCH, PIECE)
            own = array.at[0, batch, 0, rows]
            wait_bytes(own, a_recv.at[kind, piece])
            for step, slot in ((2, 3), (1, 1), (3, 2)) if RELAY[kind][batch] == 0 else ((1, 1), (3, 2)):
                remote(
                    own, array.at[0, batch, slot, rows],
                    y_send.at[kind - 1], y_recv.at[kind - 1, batch, slot - 1], ring[step],
                )

    def relay(array, kind, batch):
        slot = RELAY[kind][batch]
        if slot:
            wait_bytes(array.at[0, batch, slot], y_recv.at[kind - 1, batch, slot - 1])
            remote(
                array.at[0, batch, slot], array.at[0, batch, 3],
                y_send.at[kind - 1], y_recv.at[kind - 1, batch, 2], ring[1 if slot == 1 else 3],
            )

    def gathered(array, kind, batch):
        for slot in (1, 2, 3):
            if slot != RELAY[kind][batch]:
                wait_bytes(array.at[0, batch, slot], y_recv.at[kind - 1, batch, slot - 1])
        remote(array.at[0, batch], array.at[1, batch], s_send.at[kind - 1], s_recv.at[kind - 1, batch], sibling)

    for batch in range(batches):
        spread(v_all, 2, batch)
    for batch in range(batches):
        spread(k_all, 1, batch)
        relay(v_all, 2, batch)

    for piece in range(heads // PIECE):
        wait_bytes(q_land.at[pl.ds(piece * PIECE, PIECE)], a_recv.at[0, piece])
    query = q_land[...].reshape(keys, HEAD_DIM)
    to_exponent = math.log2(math.e) * HEAD_DIM ** (-0.5)

    def absorb(state, blocks):
        for half, batch in blocks:
            if half:
                wait_bytes(v_all.at[1, batch], s_recv.at[1, batch])
                wait_bytes(k_all.at[1, batch], s_recv.at[0, batch])
        scores = [
            lax.dot_general(
                query, k_all[half, batch].reshape(-1, HEAD_DIM), (((1,), (1,)), ((), ())),
                preferred_element_type=jnp.float32,
            )
            for half, batch in blocks
        ]
        top = jnp.max(functools.reduce(jnp.maximum, scores), axis=1, keepdims=True)
        if state is not None:
            top = jnp.maximum(top, state[0])
        exponents = [jnp.exp2((block - top) * to_exponent) for block in scores]
        total = jnp.sum(functools.reduce(jnp.add, exponents), axis=1, keepdims=True)
        mixed = functools.reduce(jnp.add, [
            jnp.dot(
                weights.astype(jnp.bfloat16), v_all[half, batch].reshape(-1, HEAD_DIM),
                preferred_element_type=jnp.float32,
            )
            for weights, (half, batch) in zip(exponents, blocks)
        ])
        if state is not None:
            fading = jnp.exp2((state[0] - top) * to_exponent)
            total = state[1] * fading + total
            mixed = state[2] * fading + mixed
        return top, total, mixed

    state = None
    for batch in range(batches):
        for array, kind in ((k_all, 1), (v_all, 2)):
            gathered(array, kind, batch)
        state = absorb(state, ([(1, batch - 1)] if batch else []) + [(0, batch)])
    state = absorb(state, [(1, batches - 1)])

    out_send[...] = (state[2] / state[1]).astype(jnp.bfloat16).reshape(heads, tokens, HEAD_DIM)
    for index in far_first:
        remote(out_send.at[index], out_hbm.at[:, columns(mine)], o_send, o_recv, home_peers[index])
    pltpu.make_async_copy(out_send.at[0], out_hbm.at[:, columns(mine)], o_recv).start()

    for kind in range(3):
        wait_bytes(q_land.at[pl.ds(0, heads - 1)], a_send.at[kind])
    for array, kind in ((k_all, 0), (v_all, 1)):
        wait_bytes(array.at[0, :, pl.ds(0, RING - 1)], y_send.at[kind])
        wait_bytes(array.at[1], s_send.at[kind])
    wait_bytes(q_land.at[pl.ds(0, heads - 1)], o_send)
    wait_bytes(out_hbm, o_recv)


def on_device(queries, keys, values, q_gain, k_gain):
    tokens, features = queries.shape
    heads = features // HEAD_DIM
    batches = heads // BATCH
    bf16 = jnp.bfloat16
    in_hbm = pl.BlockSpec(memory_space=pltpu.HBM)
    return pl.pallas_call(
        kernel,
        out_shape=jax.ShapeDtypeStruct((tokens, features), bf16),
        in_specs=[in_hbm] * 5,
        out_specs=pl.BlockSpec(memory_space=pltpu.VMEM),
        scratch_shapes=[
            pltpu.VMEM((tokens, features), bf16),
            pltpu.VMEM((tokens, features), bf16),
            pltpu.VMEM((tokens, features), bf16),
            pltpu.VMEM((heads, HEAD_DIM), jnp.float32),
            pltpu.VMEM((heads, HEAD_DIM), jnp.float32),
            pltpu.VMEM((2, tokens, HEAD_DIM), jnp.float32),
            pltpu.VMEM((heads, tokens, HEAD_DIM), bf16),
            pltpu.VMEM((heads, tokens, HEAD_DIM), bf16),
            pltpu.VMEM((heads, tokens, HEAD_DIM), bf16),
            pltpu.VMEM((CORES, batches, RING, BATCH, tokens, HEAD_DIM), bf16),
            pltpu.VMEM((CORES, batches, RING, BATCH, tokens, HEAD_DIM), bf16),
            pltpu.VMEM((heads, tokens, HEAD_DIM), bf16),
            pltpu.SemaphoreType.DMA((5,)),
            pltpu.SemaphoreType.DMA((2,)),
            pltpu.SemaphoreType.DMA((3,)),
            pltpu.SemaphoreType.DMA((3, heads // PIECE)),
            pltpu.SemaphoreType.DMA((2,)),
            pltpu.SemaphoreType.DMA((2, batches, RING - 1)),
            pltpu.SemaphoreType.DMA((2,)),
            pltpu.SemaphoreType.DMA((2, batches)),
            pltpu.SemaphoreType.DMA,
            pltpu.SemaphoreType.DMA,
        ],
        compiler_params=pltpu.CompilerParams(
            collective_id=0, has_side_effects=True, vmem_limit_bytes=40 * 1024 * 1024
        ),
    )(*(
        pltpu.with_memory_space_constraint(array, pltpu.HBM)
        for array in (queries, keys, values, q_gain.reshape(heads, HEAD_DIM), k_gain.reshape(heads, HEAD_DIM))
    ))


def solution(mesh):
    in_specs = (P("seq", "role"), P("seq", "role"), P("seq", "role"), P("role"), P("role"))
    out_specs = P("seq", "role")
    return jax.shard_map(
        on_device, mesh=mesh, in_specs=in_specs, out_specs=out_specs, check_vma=False
    )
```

```python
import functools
import math

import jax
import jax.numpy as jnp
from jax import lax
from jax.experimental import pallas as pl
from jax.experimental.pallas import tpu as pltpu
from jax.sharding import PartitionSpec as P

HEADS = 32
HEAD_DIM = 128
GRID_H = 30
GRID_W = 52
DEPTH = 8
CORES = 2
RING = 4
PLACES = CORES * RING
BATCH = 4
OFFSETS = (
    (0, 0), (1, 0), (7, 0), (0, 1),
    (2, 0), (6, 0), (1, 1), (7, 1),
    (3, 0), (5, 0), (2, 1), (6, 1),
    (4, 0), (3, 1), (5, 1), (4, 1),
)
PIECE = 2
RELAY = (None, (0, 0, 0, 0), (1, 2, 1, 2))
MESH = pl.DeviceIdType.MESH


def angle_tables(first, rows):
    half_dim = HEAD_DIM // 2
    row_pairs = HEAD_DIM // 6
    time_pairs = half_dim - 2 * row_pairs
    lane = lax.broadcasted_iota(jnp.int32, (rows, HEAD_DIM), 1)
    pair = jnp.where(lane < half_dim, lane, lane - half_dim).astype(jnp.float32)
    position = (first + lax.broadcasted_iota(jnp.int32, (rows, HEAD_DIM), 0)).astype(jnp.float32)
    grid_row = jnp.floor((position + 0.5) / GRID_W)
    column = position - GRID_W * grid_row
    frame = jnp.floor((grid_row + 0.5) / GRID_H)
    row = grid_row - GRID_H * frame
    in_frames = pair < time_pairs
    in_rows = jnp.logical_and(pair >= time_pairs, pair < time_pairs + row_pairs)
    local = jnp.where(in_frames, pair, jnp.where(in_rows, pair - time_pairs, pair - time_pairs - row_pairs))
    width = jnp.where(in_frames, jnp.float32(2 * time_pairs), jnp.float32(2 * row_pairs))
    frequency = jnp.exp(-jnp.float32(math.log(10000.0)) * 2.0 * local / width)
    coordinate = jnp.where(in_frames, frame, jnp.where(in_rows, row, column))
    angle = coordinate * frequency
    sine = jnp.sin(angle)
    return jnp.cos(angle), jnp.where(lane < half_dim, -sine, sine)


def kernel(
    q_hbm, k_hbm, v_hbm, q_gain_hbm, k_gain_hbm, out_hbm,
    q_in, k_in, v_in, q_gain, k_gain, sums, q_send, k_send, q_land, k_all, v_all, out_send,
    in_sem, sum_sem, a_send, a_recv, y_send, y_recv, s_send, s_recv, o_send, o_recv,
):
    role = lax.axis_index("role")
    seq = lax.axis_index("seq")
    tokens = q_in.shape[0]
    heads = q_send.shape[0]
    keys = heads * tokens
    mine = seq // PLACES
    place = seq % PLACES
    z = mine // 2
    x = mine % 2
    y = place // CORES
    core = place % CORES

    loads = [
        pltpu.make_async_copy(source, target, in_sem.at[index])
        for index, (source, target) in enumerate(
            ((q_hbm, q_in), (k_hbm, k_in), (k_gain_hbm, k_gain), (q_gain_hbm, q_gain), (v_hbm, v_in))
        )
    ]
    for load in loads:
        load.start()

    def home(index):
        dz, dx = OFFSETS[index]
        return lax.rem(z + dz, DEPTH) * 2 + (1 - x if dx else x)

    def server(index):
        dz, dx = OFFSETS[index]
        return lax.rem(z + DEPTH - dz, DEPTH) * 2 + (1 - x if dx else x)

    def peer(index):
        return (role, index * PLACES + place)

    def across(step):
        return (role, mine * PLACES + lax.rem(y + step, RING) * CORES + core)

    sibling = (role, mine * PLACES + y * CORES + 1 - core)
    partner = (1 - role, seq)
    far_first = range(heads - 1, 0, -1)
    servers = [server(index) for index in range(heads)]
    homes = [home(index) for index in range(heads)]
    server_peers = [peer(index) for index in servers]
    home_peers = [peer(index) for index in homes]
    ring = [across(step) for step in range(RING)]

    barrier = pltpu.get_barrier_semaphore()
    for index in far_first:
        pl.semaphore_signal(barrier, inc=1, device_id=server_peers[index], device_id_type=MESH)
    for other in (partner, sibling, ring[1], ring[2], ring[3]):
        pl.semaphore_signal(barrier, inc=1, device_id=other, device_id_type=MESH)
    loads[0].wait()
    loads[1].wait()

    def square_sum(ref):
        total = jnp.zeros((tokens, HEAD_DIM), jnp.float32)
        for head in range(heads):
            rows = ref[:, head * HEAD_DIM:(head + 1) * HEAD_DIM].astype(jnp.float32)
            total = total + rows * rows
        return jnp.sum(total, axis=1, keepdims=True)

    lane = lax.broadcasted_iota(jnp.int32, (tokens, HEAD_DIM), 1)
    sums[0] = jnp.where(lane < HEAD_DIM // 2, square_sum(q_in), square_sum(k_in))
    cosine, sine = angle_tables(seq * tokens, tokens)
    loads[2].wait()
    loads[3].wait()
    loads[4].wait()
    pl.semaphore_wait(barrier, heads + RING)

    def columns(index):
        return pl.ds(pl.multiple_of(index * HEAD_DIM, HEAD_DIM), HEAD_DIM)

    def remote(source, target, send_sem, recv_sem, device):
        pltpu.make_async_remote_copy(
            src_ref=source, dst_ref=target, send_sem=send_sem, recv_sem=recv_sem, device_id=device, device_id_type=MESH
        ).start()

    def wait_bytes(ref, sem):
        pltpu.make_async_copy(ref, ref, sem).wait()

    def exchange(pick, slot, kind):
        for index in far_first:
            remote(
                pick(servers[index]), slot(index), a_send.at[kind], a_recv.at[kind, index // PIECE],
                server_peers[index],
            )
        pltpu.make_async_copy(pick(mine), slot(0), a_recv.at[kind, 0]).start()

    exchange(lambda to: v_in.at[:, columns(to)], lambda i: v_all.at[0, i // BATCH, 0, i % BATCH], 2)

    sum_copy = pltpu.make_async_remote_copy(
        src_ref=sums.at[0], dst_ref=sums.at[1], send_sem=sum_sem.at[0], recv_sem=sum_sem.at[1],
        device_id=partner, device_id_type=MESH,
    )
    sum_copy.start()
    sum_copy.wait()
    scale = lax.rsqrt((sums[0] + sums[1]) / (HEADS * HEAD_DIM) + 1e-06)

    def prepare(source, factor, gain, target):
        for head in range(heads):
            rows = source[:, head * HEAD_DIM:(head + 1) * HEAD_DIM].astype(jnp.float32)
            rows = rows * factor * gain[head:head + 1, :]
            rows = rows * cosine + pltpu.roll(rows, HEAD_DIM // 2, 1) * sine
            target[head] = rows.astype(jnp.bfloat16)

    prepare(k_in, scale[:, HEAD_DIM // 2:HEAD_DIM // 2 + 1], k_gain, k_send)
    exchange(lambda to: k_send.at[to], lambda i: k_all.at[0, i // BATCH, 0, i % BATCH], 1)
    prepare(q_in, scale[:, 0:1], q_gain, q_send)
    exchange(lambda to: q_send.at[to], lambda i: q_land.at[i], 0)

    batches = heads // BATCH

    def spread(array, kind, batch):
        for piece in range(batch * BATCH // PIECE, (batch + 1) * BATCH // PIECE):
            rows = pl.ds(piece * PIECE % BATCH, PIECE)
            own = array.at[0, batch, 0, rows]
            wait_bytes(own, a_recv.at[kind, piece])
            for step, slot in ((2, 3), (1, 1), (3, 2)) if RELAY[kind][batch] == 0 else ((1, 1), (3, 2)):
                remote(
                    own, array.at[0, batch, slot, rows],
                    y_send.at[kind - 1], y_recv.at[kind - 1, batch, slot - 1], ring[step],
                )

    def relay(array, kind, batch):
        slot = RELAY[kind][batch]
        if slot:
            wait_bytes(array.at[0, batch, slot], y_recv.at[kind - 1, batch, slot - 1])
            remote(
                array.at[0, batch, slot], array.at[0, batch, 3],
                y_send.at[kind - 1], y_recv.at[kind - 1, batch, 2], ring[1 if slot == 1 else 3],
            )

    def gathered(array, kind, batch):
        for slot in (1, 2, 3):
            if slot != RELAY[kind][batch]:
                wait_bytes(array.at[0, batch, slot], y_recv.at[kind - 1, batch, slot - 1])
        remote(array.at[0, batch], array.at[1, batch], s_send.at[kind - 1], s_recv.at[kind - 1, batch], sibling)

    for batch in range(batches):
        spread(v_all, 2, batch)
    for batch in range(batches):
        spread(k_all, 1, batch)
        relay(v_all, 2, batch)

    for piece in range(heads // PIECE):
        wait_bytes(q_land.at[pl.ds(piece * PIECE, PIECE)], a_recv.at[0, piece])
    query = q_land[...].reshape(keys, HEAD_DIM)
    to_exponent = math.log2(math.e) * HEAD_DIM ** (-0.5)

    def absorb(state, query, blocks, ready=False):
        for half, batch in blocks:
            if half and not ready:
                wait_bytes(v_all.at[1, batch], s_recv.at[1, batch])
                wait_bytes(k_all.at[1, batch], s_recv.at[0, batch])
        scores = [
            lax.dot_general(
                query, k_all[half, batch].reshape(-1, HEAD_DIM), (((1,), (1,)), ((), ())),
                preferred_element_type=jnp.float32,
            )
            for half, batch in blocks
        ]
        top = jnp.max(functools.reduce(jnp.maximum, scores), axis=1, keepdims=True)
        if state is not None:
            top = jnp.maximum(top, state[0])
        exponents = [jnp.exp2((block - top) * to_exponent) for block in scores]
        total = jnp.sum(functools.reduce(jnp.add, exponents), axis=1, keepdims=True)
        mixed = functools.reduce(jnp.add, [
            jnp.dot(
                weights.astype(jnp.bfloat16), v_all[half, batch].reshape(-1, HEAD_DIM),
                preferred_element_type=jnp.float32,
            )
            for weights, (half, batch) in zip(exponents, blocks)
        ])
        if state is not None:
            fading = jnp.exp2((state[0] - top) * to_exponent)
            total = state[1] * fading + total
            mixed = state[2] * fading + mixed
        return top, total, mixed

    state = None
    for batch in range(batches):
        for array, kind in ((k_all, 1), (v_all, 2)):
            gathered(array, kind, batch)
        state = absorb(state, query, ([(1, batch - 1)] if batch else []) + [(0, batch)])
    middle = heads // 2
    for first in (middle, 0):
        rows = slice(first * tokens, (first + middle) * tokens)
        _, total, mixed = absorb(
            tuple(part[rows] for part in state), query[rows], [(1, batches - 1)], ready=first == 0
        )
        out_send[first:first + middle] = (mixed / total).astype(jnp.bfloat16).reshape(middle, tokens, HEAD_DIM)
        for index in range(first + middle - 1, max(first, 1) - 1, -1):
            remote(out_send.at[index], out_hbm.at[:, columns(mine)], o_send, o_recv, home_peers[index])
    pltpu.make_async_copy(out_send.at[0], out_hbm.at[:, columns(mine)], o_recv).start()

    for kind in range(3):
        wait_bytes(q_land.at[pl.ds(0, heads - 1)], a_send.at[kind])
    for array, kind in ((k_all, 0), (v_all, 1)):
        wait_bytes(array.at[0, :, pl.ds(0, RING - 1)], y_send.at[kind])
        wait_bytes(array.at[1], s_send.at[kind])
    wait_bytes(q_land.at[pl.ds(0, heads - 1)], o_send)
    wait_bytes(out_hbm, o_recv)


def on_device(queries, keys, values, q_gain, k_gain):
    tokens, features = queries.shape
    heads = features // HEAD_DIM
    batches = heads // BATCH
    bf16 = jnp.bfloat16
    in_hbm = pl.BlockSpec(memory_space=pltpu.HBM)
    return pl.pallas_call(
        kernel,
        out_shape=jax.ShapeDtypeStruct((tokens, features), bf16),
        in_specs=[in_hbm] * 5,
        out_specs=pl.BlockSpec(memory_space=pltpu.VMEM),
        scratch_shapes=[
            pltpu.VMEM((tokens, features), bf16),
            pltpu.VMEM((tokens, features), bf16),
            pltpu.VMEM((tokens, features), bf16),
            pltpu.VMEM((heads, HEAD_DIM), jnp.float32),
            pltpu.VMEM((heads, HEAD_DIM), jnp.float32),
            pltpu.VMEM((2, tokens, HEAD_DIM), jnp.float32),
            pltpu.VMEM((heads, tokens, HEAD_DIM), bf16),
            pltpu.VMEM((heads, tokens, HEAD_DIM), bf16),
            pltpu.VMEM((heads, tokens, HEAD_DIM), bf16),
            pltpu.VMEM((CORES, batches, RING, BATCH, tokens, HEAD_DIM), bf16),
            pltpu.VMEM((CORES, batches, RING, BATCH, tokens, HEAD_DIM), bf16),
            pltpu.VMEM((heads, tokens, HEAD_DIM), bf16),
            pltpu.SemaphoreType.DMA((5,)),
            pltpu.SemaphoreType.DMA((2,)),
            pltpu.SemaphoreType.DMA((3,)),
            pltpu.SemaphoreType.DMA((3, heads // PIECE)),
            pltpu.SemaphoreType.DMA((2,)),
            pltpu.SemaphoreType.DMA((2, batches, RING - 1)),
            pltpu.SemaphoreType.DMA((2,)),
            pltpu.SemaphoreType.DMA((2, batches)),
            pltpu.SemaphoreType.DMA,
            pltpu.SemaphoreType.DMA,
        ],
        compiler_params=pltpu.CompilerParams(
            collective_id=0, has_side_effects=True, vmem_limit_bytes=40 * 1024 * 1024
        ),
    )(*(
        pltpu.with_memory_space_constraint(array, pltpu.HBM)
        for array in (queries, keys, values, q_gain.reshape(heads, HEAD_DIM), k_gain.reshape(heads, HEAD_DIM))
    ))


def solution(mesh):
    in_specs = (P("seq", "role"), P("seq", "role"), P("seq", "role"), P("role"), P("role"))
    out_specs = P("seq", "role")
    return jax.shard_map(
        on_device, mesh=mesh, in_specs=in_specs, out_specs=out_specs, check_vma=False
    )
```

```python
import functools
import math

import jax
import jax.numpy as jnp
from jax import lax
from jax.experimental import pallas as pl
from jax.experimental.pallas import tpu as pltpu
from jax.sharding import PartitionSpec as P

HEADS = 32
HEAD_DIM = 128
GRID_H = 30
GRID_W = 52
DEPTH = 8
CORES = 2
RING = 4
PLACES = CORES * RING
BATCH = 4
OFFSETS = (
    (0, 0), (1, 0), (7, 0), (0, 1),
    (2, 0), (6, 0), (1, 1), (7, 1),
    (3, 0), (5, 0), (2, 1), (6, 1),
    (4, 0), (3, 1), (5, 1), (4, 1),
)
PIECE = 2
RELAY = (None, (0, 0, 0, 0), (1, 2, 1, 2))
MESH = pl.DeviceIdType.MESH


def angle_tables(first, rows):
    half_dim = HEAD_DIM // 2
    row_pairs = HEAD_DIM // 6
    time_pairs = half_dim - 2 * row_pairs
    lane = lax.broadcasted_iota(jnp.int32, (rows, HEAD_DIM), 1)
    pair = jnp.where(lane < half_dim, lane, lane - half_dim).astype(jnp.float32)
    position = (first + lax.broadcasted_iota(jnp.int32, (rows, HEAD_DIM), 0)).astype(jnp.float32)
    grid_row = jnp.floor((position + 0.5) / GRID_W)
    column = position - GRID_W * grid_row
    frame = jnp.floor((grid_row + 0.5) / GRID_H)
    row = grid_row - GRID_H * frame
    in_frames = pair < time_pairs
    in_rows = jnp.logical_and(pair >= time_pairs, pair < time_pairs + row_pairs)
    local = jnp.where(in_frames, pair, jnp.where(in_rows, pair - time_pairs, pair - time_pairs - row_pairs))
    width = jnp.where(in_frames, jnp.float32(2 * time_pairs), jnp.float32(2 * row_pairs))
    frequency = jnp.exp(-jnp.float32(math.log(10000.0)) * 2.0 * local / width)
    coordinate = jnp.where(in_frames, frame, jnp.where(in_rows, row, column))
    angle = coordinate * frequency
    sine = jnp.sin(angle)
    return jnp.cos(angle), jnp.where(lane < half_dim, -sine, sine)


def kernel(
    q_hbm, k_hbm, v_hbm, q_gain_hbm, k_gain_hbm, out_hbm,
    q_in, k_in, v_in, q_gain, k_gain, sums, q_send, k_send, q_land, k_all, v_all, out_send,
    in_sem, sum_sem, a_send, a_recv, y_send, y_recv, s_send, s_recv, o_send, o_recv,
):
    role = lax.axis_index("role")
    seq = lax.axis_index("seq")
    tokens = q_in.shape[0]
    heads = q_send.shape[0]
    keys = heads * tokens
    mine = seq // PLACES
    place = seq % PLACES
    z = mine // 2
    x = mine % 2
    y = place // CORES
    core = place % CORES

    loads = [
        pltpu.make_async_copy(source, target, in_sem.at[index])
        for index, (source, target) in enumerate(
            ((q_hbm, q_in), (k_hbm, k_in), (k_gain_hbm, k_gain), (q_gain_hbm, q_gain), (v_hbm, v_in))
        )
    ]
    for load in loads:
        load.start()

    def home(index):
        dz, dx = OFFSETS[index]
        return lax.rem(z + dz, DEPTH) * 2 + (1 - x if dx else x)

    def server(index):
        dz, dx = OFFSETS[index]
        return lax.rem(z + DEPTH - dz, DEPTH) * 2 + (1 - x if dx else x)

    def peer(index):
        return (role, index * PLACES + place)

    def across(step):
        return (role, mine * PLACES + lax.rem(y + step, RING) * CORES + core)

    sibling = (role, mine * PLACES + y * CORES + 1 - core)
    partner = (1 - role, seq)
    far_first = range(heads - 1, 0, -1)
    servers = [server(index) for index in range(heads)]
    homes = [home(index) for index in range(heads)]
    server_peers = [peer(index) for index in servers]
    home_peers = [peer(index) for index in homes]
    ring = [across(step) for step in range(RING)]

    barrier = pltpu.get_barrier_semaphore()
    for index in far_first:
        pl.semaphore_signal(barrier, inc=1, device_id=server_peers[index], device_id_type=MESH)
    for other in (partner, sibling, ring[1], ring[2], ring[3]):
        pl.semaphore_signal(barrier, inc=1, device_id=other, device_id_type=MESH)
    loads[0].wait()
    loads[1].wait()

    def square_sum(ref):
        total = jnp.zeros((tokens, HEAD_DIM), jnp.float32)
        for head in range(heads):
            rows = ref[:, head * HEAD_DIM:(head + 1) * HEAD_DIM].astype(jnp.float32)
            total = total + rows * rows
        return jnp.sum(total, axis=1, keepdims=True)

    lane = lax.broadcasted_iota(jnp.int32, (tokens, HEAD_DIM), 1)
    sums[0] = jnp.where(lane < HEAD_DIM // 2, square_sum(q_in), square_sum(k_in))
    cosine, sine = angle_tables(seq * tokens, tokens)
    loads[2].wait()
    loads[3].wait()
    loads[4].wait()
    pl.semaphore_wait(barrier, heads + RING)

    def columns(index):
        return pl.ds(pl.multiple_of(index * HEAD_DIM, HEAD_DIM), HEAD_DIM)

    def remote(source, target, send_sem, recv_sem, device):
        pltpu.make_async_remote_copy(
            src_ref=source, dst_ref=target, send_sem=send_sem, recv_sem=recv_sem, device_id=device, device_id_type=MESH
        ).start()

    def wait_bytes(ref, sem):
        pltpu.make_async_copy(ref, ref, sem).wait()

    def exchange(pick, slot, kind, chosen=far_first):
        for index in chosen:
            remote(
                pick(servers[index]), slot(index), a_send.at[kind], a_recv.at[kind, index // PIECE],
                server_peers[index],
            )
        if 1 in chosen:
            pltpu.make_async_copy(pick(mine), slot(0), a_recv.at[kind, 0]).start()

    exchange(lambda to: v_in.at[:, columns(to)], lambda i: v_all.at[0, i // BATCH, 0, i % BATCH], 2)

    sum_copy = pltpu.make_async_remote_copy(
        src_ref=sums.at[0], dst_ref=sums.at[1], send_sem=sum_sem.at[0], recv_sem=sum_sem.at[1],
        device_id=partner, device_id_type=MESH,
    )
    sum_copy.start()
    sum_copy.wait()
    scale = lax.rsqrt((sums[0] + sums[1]) / (HEADS * HEAD_DIM) + 1e-06)

    def prepare(source, factor, gain, target, chosen):
        for index in chosen:
            head = servers[index]
            rows = source[:, columns(head)].astype(jnp.float32)
            rows = rows * factor * gain[pl.ds(head, 1), :]
            rows = rows * cosine + pltpu.roll(rows, HEAD_DIM // 2, 1) * sine
            target[head] = rows.astype(jnp.bfloat16)

    half = heads // 2
    key_scale = scale[:, HEAD_DIM // 2:HEAD_DIM // 2 + 1]
    for chosen in (range(heads - 1, half - 1, -1), range(half - 1, -1, -1)):
        prepare(k_in, key_scale, k_gain, k_send, chosen)
        sent = [index for index in chosen if index]
        exchange(lambda to: k_send.at[to], lambda i: k_all.at[0, i // BATCH, 0, i % BATCH], 1, sent)
    prepare(q_in, scale[:, 0:1], q_gain, q_send, range(heads))
    exchange(lambda to: q_send.at[to], lambda i: q_land.at[i], 0)

    batches = heads // BATCH

    def spread(array, kind, batch):
        for piece in range(batch * BATCH // PIECE, (batch + 1) * BATCH // PIECE):
            rows = pl.ds(piece * PIECE % BATCH, PIECE)
            own = array.at[0, batch, 0, rows]
            wait_bytes(own, a_recv.at[kind, piece])
            for step, slot in ((2, 3), (1, 1), (3, 2)) if RELAY[kind][batch] == 0 else ((1, 1), (3, 2)):
                remote(
                    own, array.at[0, batch, slot, rows],
                    y_send.at[kind - 1], y_recv.at[kind - 1, batch, slot - 1], ring[step],
                )

    def relay(array, kind, batch):
        slot = RELAY[kind][batch]
        if slot:
            wait_bytes(array.at[0, batch, slot], y_recv.at[kind - 1, batch, slot - 1])
            remote(
                array.at[0, batch, slot], array.at[0, batch, 3],
                y_send.at[kind - 1], y_recv.at[kind - 1, batch, 2], ring[1 if slot == 1 else 3],
            )

    def gathered(array, kind, batch):
        for slot in (1, 2, 3):
            if slot != RELAY[kind][batch]:
                wait_bytes(array.at[0, batch, slot], y_recv.at[kind - 1, batch, slot - 1])
        remote(array.at[0, batch], array.at[1, batch], s_send.at[kind - 1], s_recv.at[kind - 1, batch], sibling)

    for batch in range(batches):
        spread(v_all, 2, batch)
    for batch in range(batches):
        spread(k_all, 1, batch)
        relay(v_all, 2, batch)

    for piece in range(heads // PIECE):
        wait_bytes(q_land.at[pl.ds(piece * PIECE, PIECE)], a_recv.at[0, piece])
    query = q_land[...].reshape(keys, HEAD_DIM)
    to_exponent = math.log2(math.e) * HEAD_DIM ** (-0.5)

    def absorb(state, query, blocks, ready=False):
        for half, batch in blocks:
            if half and not ready:
                wait_bytes(v_all.at[1, batch], s_recv.at[1, batch])
                wait_bytes(k_all.at[1, batch], s_recv.at[0, batch])
        scores = [
            lax.dot_general(
                query, k_all[half, batch].reshape(-1, HEAD_DIM), (((1,), (1,)), ((), ())),
                preferred_element_type=jnp.float32,
            )
            for half, batch in blocks
        ]
        top = jnp.max(functools.reduce(jnp.maximum, scores), axis=1, keepdims=True)
        if state is not None:
            top = jnp.maximum(top, state[0])
        exponents = [jnp.exp2((block - top) * to_exponent) for block in scores]
        total = jnp.sum(functools.reduce(jnp.add, exponents), axis=1, keepdims=True)
        mixed = functools.reduce(jnp.add, [
            jnp.dot(
                weights.astype(jnp.bfloat16), v_all[half, batch].reshape(-1, HEAD_DIM),
                preferred_element_type=jnp.float32,
            )
            for weights, (half, batch) in zip(exponents, blocks)
        ])
        if state is not None:
            fading = jnp.exp2((state[0] - top) * to_exponent)
            total = state[1] * fading + total
            mixed = state[2] * fading + mixed
        return top, total, mixed

    state = None
    for batch in range(batches):
        for array, kind in ((k_all, 1), (v_all, 2)):
            gathered(array, kind, batch)
        state = absorb(state, query, ([(1, batch - 1)] if batch else []) + [(0, batch)])
    middle = heads // 2
    for first in (middle, 0):
        rows = slice(first * tokens, (first + middle) * tokens)
        _, total, mixed = absorb(
            tuple(part[rows] for part in state), query[rows], [(1, batches - 1)], ready=first == 0
        )
        out_send[first:first + middle] = (mixed / total).astype(jnp.bfloat16).reshape(middle, tokens, HEAD_DIM)
        for index in range(first + middle - 1, max(first, 1) - 1, -1):
            remote(out_send.at[index], out_hbm.at[:, columns(mine)], o_send, o_recv, home_peers[index])
    pltpu.make_async_copy(out_send.at[0], out_hbm.at[:, columns(mine)], o_recv).start()

    for kind in range(3):
        wait_bytes(q_land.at[pl.ds(0, heads - 1)], a_send.at[kind])
    for array, kind in ((k_all, 0), (v_all, 1)):
        wait_bytes(array.at[0, :, pl.ds(0, RING - 1)], y_send.at[kind])
        wait_bytes(array.at[1], s_send.at[kind])
    wait_bytes(q_land.at[pl.ds(0, heads - 1)], o_send)
    wait_bytes(out_hbm, o_recv)


def on_device(queries, keys, values, q_gain, k_gain):
    tokens, features = queries.shape
    heads = features // HEAD_DIM
    batches = heads // BATCH
    bf16 = jnp.bfloat16
    in_hbm = pl.BlockSpec(memory_space=pltpu.HBM)
    return pl.pallas_call(
        kernel,
        out_shape=jax.ShapeDtypeStruct((tokens, features), bf16),
        in_specs=[in_hbm] * 5,
        out_specs=pl.BlockSpec(memory_space=pltpu.VMEM),
        scratch_shapes=[
            pltpu.VMEM((tokens, features), bf16),
            pltpu.VMEM((tokens, features), bf16),
            pltpu.VMEM((tokens, features), bf16),
            pltpu.VMEM((heads, HEAD_DIM), jnp.float32),
            pltpu.VMEM((heads, HEAD_DIM), jnp.float32),
            pltpu.VMEM((2, tokens, HEAD_DIM), jnp.float32),
            pltpu.VMEM((heads, tokens, HEAD_DIM), bf16),
            pltpu.VMEM((heads, tokens, HEAD_DIM), bf16),
            pltpu.VMEM((heads, tokens, HEAD_DIM), bf16),
            pltpu.VMEM((CORES, batches, RING, BATCH, tokens, HEAD_DIM), bf16),
            pltpu.VMEM((CORES, batches, RING, BATCH, tokens, HEAD_DIM), bf16),
            pltpu.VMEM((heads, tokens, HEAD_DIM), bf16),
            pltpu.SemaphoreType.DMA((5,)),
            pltpu.SemaphoreType.DMA((2,)),
            pltpu.SemaphoreType.DMA((3,)),
            pltpu.SemaphoreType.DMA((3, heads // PIECE)),
            pltpu.SemaphoreType.DMA((2,)),
            pltpu.SemaphoreType.DMA((2, batches, RING - 1)),
            pltpu.SemaphoreType.DMA((2,)),
            pltpu.SemaphoreType.DMA((2, batches)),
            pltpu.SemaphoreType.DMA,
            pltpu.SemaphoreType.DMA,
        ],
        compiler_params=pltpu.CompilerParams(
            collective_id=0, has_side_effects=True, vmem_limit_bytes=40 * 1024 * 1024
        ),
    )(*(
        pltpu.with_memory_space_constraint(array, pltpu.HBM)
        for array in (queries, keys, values, q_gain.reshape(heads, HEAD_DIM), k_gain.reshape(heads, HEAD_DIM))
    ))


def solution(mesh):
    in_specs = (P("seq", "role"), P("seq", "role"), P("seq", "role"), P("role"), P("role"))
    out_specs = P("seq", "role")
    return jax.shard_map(
        on_device, mesh=mesh, in_specs=in_specs, out_specs=out_specs, check_vma=False
    )
```
